512 devices in a mesh: fsdp: 32 (over y, z_hi, core), tp: 16 (over x, z_lo).
Axes of the slice: x: 4, y: 4, z: 16 (z_hi: 4, z_lo: 4; z = z_hi * 4 + z_lo), core: 2. Of those that a mesh axis runs over, the one named last changes fastest.
Arguments:
- tokens: bfloat16 [16384, 8192], P('fsdp', 'tp'), may hold values from -12 to 12
- fixed_query_weight: bfloat16 [8192, 8192], P('fsdp', 'tp'), may hold values from -0.0625 to 0.0625
- adapter_down_factor: bfloat16 [8, 8192], P(None, 'fsdp'), may hold values from -0.0625 to 0.0625
- adapter_up_factor: bfloat16 [8, 8192], P(None, 'tp'), may hold values from -0.125 to 0.125
- cotangent: bfloat16 [16384, 8192], P('fsdp', 'tp'), may hold values from -24 to 24
- importance: float32 [8192, 8192], P('fsdp', 'tp'), may hold values from 0.05 to 0.5
Outputs:
- projected: bfloat16 [16384, 8192], P('fsdp', 'tp')
- up_factor_gradient: float32 [8, 8192], P(None, 'tp')
- down_factor_gradient: float32 [8, 8192], P(None, 'fsdp')
- new_importance: float32 [8192, 8192], P('fsdp', 'tp')
The draws below stay inside these ranges and needn't reach their ends.
All inputs are finite; a program needn't handle non-finite values.
Results may differ from the reference program's by a relative error of at most 0.0029.
Values may be sent and summed in bfloat16 or wider, within the bound.
A program may use at most 64 MiB of HBM per device.

```python
import math
import jax
import jax.numpy as jnp
from jax import lax

MODEL_WIDTH = 8192
ADAPTER_RANK = 8
TOKENS = 16384


def with_spikes(values, stream_key, source, target, shards_of, factor):
    def block_of(position):
        return (jnp.arange(values.shape[position]) // (values.shape[position] // shards_of)).reshape((-1,) + (1,) * (values.ndim - 1 - position))

    first = jax.random.permutation(stream_key, shards_of)[block_of(target)]
    other_side = (block_of(target) + shards_of // 2) % shards_of
    return jnp.where((block_of(source) == first) | (block_of(source) == other_side), factor * values, values)


def steps_of(stream_key, shape, shards, least, high):
    def one(dim, shards_of):
        steps = jax.random.uniform(jax.random.fold_in(jax.random.fold_in(stream_key, 6), dim), (shards_of,), jnp.float32, least / len(shards), high / len(shards))
        return jnp.repeat(jnp.exp(steps), shape[dim] // shards_of).reshape((-1,) + (1,) * (len(shape) - dim - 1))

    level = one(*shards[0])
    for cut in shards[1:]:
        level = level * one(*cut)
    return level


def normal_values(stream_key, shape, deviation, limit, pieces=(), kind=jnp.bfloat16):
    result = jax.random.normal(stream_key, shape, jnp.float32) * deviation
    if len(pieces) > 0:
        result = steps_of(stream_key, shape, pieces, -0.22, 0.18) * result
    return jnp.clip(result, min=-limit, max=limit).astype(kind)


def heavy_noise(key, extent, spread, most, pieces, heavy, dtype=jnp.bfloat16):
    result = spread * jax.random.normal(key, extent, jnp.float32)
    if pieces:
        result = result * steps_of(key, extent, pieces, -0.22, 0.18)
    return jnp.clip(with_spikes(result, jax.random.fold_in(key, 3), *heavy), -most, most).astype(dtype)


def setup_inputs(seed: int = 0) -> dict:
    arg_keys = jax.random.split(jax.random.key(seed), 7)
    return {
        "tokens": heavy_noise(arg_keys[0], (TOKENS, MODEL_WIDTH), 1.0, 12.0, ((0, 32), (1, 16)), (0, 1, 32, 2.75)),
        "fixed_query_weight": normal_values(arg_keys[1], (MODEL_WIDTH, MODEL_WIDTH), MODEL_WIDTH ** -0.5, 0.0625, ((0, 32), (1, 16))),
        "adapter_down_factor": normal_values(arg_keys[2], (ADAPTER_RANK, MODEL_WIDTH), MODEL_WIDTH ** -0.5, 0.0625, ((1, 32),)),
        "adapter_up_factor": normal_values(arg_keys[3], (ADAPTER_RANK, MODEL_WIDTH), 0.02, 0.125, ((1, 16),)),
        "cotangent": normal_values(arg_keys[4], (TOKENS, MODEL_WIDTH), 4.0, 24.0, ((0, 32), (1, 16))),
        "importance": jnp.clip(jnp.exp(math.log(0.5) - 2.3025851 * jax.random.uniform(arg_keys[5], (MODEL_WIDTH, MODEL_WIDTH), jnp.float32) ** steps_of(arg_keys[5], (MODEL_WIDTH, MODEL_WIDTH), ((0, 32), (1, 16)), -0.2, 0.2)), 0.05, 0.5),
    }


adapter_scale = 2.0
decay_rate = 0.8


def reference(tokens, fixed_query_weight, adapter_down_factor, adapter_up_factor, cotangent, importance):
    rank_activation = jnp.dot(tokens, adapter_down_factor.T, preferred_element_type=jnp.float32).astype(jnp.bfloat16)
    projected = jnp.dot(tokens, fixed_query_weight, preferred_element_type=jnp.float32)
    projected = projected + adapter_scale * jnp.dot(rank_activation, adapter_up_factor, preferred_element_type=jnp.float32)
    projected = projected.astype(jnp.bfloat16)
    up_factor_gradient = adapter_scale * jnp.dot(rank_activation.T, cotangent, preferred_element_type=jnp.float32)
    backward_product = jnp.dot(cotangent, adapter_up_factor.T, preferred_element_type=jnp.float32).astype(jnp.bfloat16)
    down_factor_gradient = adapter_scale * jnp.dot(backward_product.T, tokens, preferred_element_type=jnp.float32)
    merged_weight = fixed_query_weight.astype(jnp.float32) + adapter_scale * jnp.dot(adapter_down_factor.T, adapter_up_factor, preferred_element_type=jnp.float32)
    importance_estimate = jnp.dot(down_factor_gradient.T, adapter_up_factor.astype(jnp.float32), precision=lax.Precision.HIGHEST)
    importance_estimate = importance_estimate + jnp.dot(adapter_down_factor.astype(jnp.float32).T, up_factor_gradient, precision=lax.Precision.HIGHEST)
    new_importance = decay_rate * importance + (1.0 - decay_rate) * jnp.abs(merged_weight * importance_estimate)
    return projected, up_factor_gradient, down_factor_gradient, new_importance
```

```python
import jax
import jax.numpy as jnp
from jax import lax
from jax.experimental import pallas as pl
from jax.experimental.pallas import tpu as pltpu
from jax.sharding import PartitionSpec as P

adapter_scale = 2.0
decay_rate = 0.8
MESH = pl.DeviceIdType.MESH
WEIGHT_START = 2


def dot(a, b, dims, precision=None):
    return lax.dot_general(
        a, b, (dims, ((), ())), preferred_element_type=jnp.float32, precision=precision
    )


def kernel(
    tok_in, w_in, down, up, cot_in, imp_in,
    proj_out, upg_out, dng_out, newimp_out,
    T, W, acc, proj, cot, imp, newimp, upg, dng, down_t, dtot,
    arx, arz, arc, ary, arh,
    load_sem, store_sem,
    tx_s, tx_r, txh_s, txh_r, tz_s, tz_r,
    wz_s, wz_r, wzh_s, wzh_r, wy_s, wy_r, wyh_s, wyh_r, wc_s, wc_r,
    arx_s, arx_r, arz_s, arz_r, arc_s, arc_r, ary_s, ary_r, arh_s, arh_r,
    dt_s, dt_r, dg_s, dg_r,
):
    f = lax.axis_index("fsdp")
    t = lax.axis_index("tp")
    chip = f // 2
    c = f % 2
    y, zh = chip // 4, chip % 4
    x, zl = t // 4, t % 4

    def dev(y=y, zh=zh, c=c, x=x, zl=zl):
        return {"fsdp": (y * 4 + zh) * 2 + c, "tp": x * 4 + zl}

    def ring(i, d):
        return (i + d + 4) % 4

    x_next, x_prev = dev(x=ring(x, 1)), dev(x=ring(x, -1))
    y_next, y_prev = dev(y=ring(y, 1)), dev(y=ring(y, -1))
    h_next, h_prev = dev(zh=ring(zh, 1)), dev(zh=ring(zh, -1))
    l_next, l_prev = dev(zl=ring(zl, 1)), dev(zl=ring(zl, -1))
    sibling = dev(c=1 - c)
    off_diagonal = chip != t

    def mirror(core):
        return {"fsdp": t * 2 + core, "tp": chip}

    def remote(src, dst, send, recv, to):
        return pltpu.make_async_remote_copy(
            src_ref=src, dst_ref=dst, send_sem=send, recv_sem=recv, device_id=to, device_id_type=MESH
        )

    loads = [
        pltpu.make_async_copy(src, dst, load_sem.at[i])
        for i, (src, dst) in enumerate(
            [
                (tok_in, T.at[x, zl]),
                (w_in, W.at[y, zh, c]),
                (cot_in, cot),
                (imp_in, imp),
            ]
        )
    ]
    for load in loads:
        load.start()

    barrier = pltpu.get_barrier_semaphore()
    for r in (1, 2, 3):
        for partner in (dev(x=ring(x, r)), dev(y=ring(y, r)), dev(zh=ring(zh, r)), dev(zl=ring(zl, r))):
            pl.semaphore_signal(barrier, inc=1, device_id=partner, device_id_type=MESH)
    pl.semaphore_signal(barrier, inc=1, device_id=sibling, device_id_type=MESH)

    @pl.when(off_diagonal)
    def _():
        for core in (0, 1):
            pl.semaphore_signal(barrier, inc=1, device_id=mirror(core), device_id_type=MESH)

    for load in loads[:2]:
        load.wait()
    down_f32 = down[...].astype(jnp.float32)
    dtot[2] = down_f32
    pl.semaphore_wait(barrier, jnp.where(off_diagonal, 15, 13))

    sends = []

    def go(copy):
        copy.start()
        sends.append(copy)
        return copy

    down_away = remote(dtot.at[2], down_t.at[c], dt_s.at[0], dt_r.at[c], sibling)
    down_mirror = [
        remote(dtot.at[2], down_t.at[c], dt_s.at[1 + core], dt_r.at[c], mirror(core)) for core in (0, 1)
    ]

    @pl.when(jnp.logical_not(off_diagonal))
    def _():
        down_t[c] = down_f32
        down_away.start()

    @pl.when(off_diagonal)
    def _():
        for copy in down_mirror:
            copy.start()

    unit = [
        zl,
        jnp.where(zl == 0, 1, jnp.where(zl == 1, 0, jnp.where(zl == 2, 1, 2))),
        jnp.where(zl == 0, 2, jnp.where(zl == 1, 2, jnp.where(zl == 2, 3, 1))),
        jnp.where(zl < 2, 3, 0),
    ]
    wunit = [zh, ring(zh, -1), ring(zh, 1), ring(zh, 2)]

    def send_x(j):
        for side, to in enumerate((x_next, x_prev)):
            go(remote(T.at[x, unit[j]], T.at[x, unit[j]], tx_s.at[side, j], tx_r.at[side, j], to))

    z_forwards = []

    def send_z(j):
        block = T.at[x, unit[j]]
        if j == 0:
            cases = ((zl < 3, l_next, 0), (zl > 0, l_prev, 1))
        else:
            cases = (
                (jnp.logical_and(unit[j] < zl, zl < 3), l_next, 0),
                (jnp.logical_and(unit[j] > zl, zl > 0), l_prev, 1),
            )
        for cond, to, side in cases:
            copy = remote(block, block, tz_s.at[side, j], tz_r.at[unit[j]], to)
            z_forwards.append((cond, copy))

            @pl.when(cond)
            def _(copy=copy):
                copy.start()

    def recv(dst, sem):
        remote(dst, dst, sem, sem, sibling).wait_recv()

    def recv_z(j):
        recv(T.at[x, unit[j]], tz_r.at[unit[j]])
        send_z(j)
        send_x(j)

    half = 256

    def recv_x(j):
        left, right = ring(x, -1), ring(x, 1)
        recv(T.at[left, unit[j]], tx_r.at[0, j])
        block = T.at[left, unit[j], pl.ds(0, half)]
        go(remote(block, block, txh_s.at[0, j], txh_r.at[0, j], x_next))
        recv(T.at[right, unit[j]], tx_r.at[1, j])
        block = T.at[right, unit[j], pl.ds(half, half)]
        go(remote(block, block, txh_s.at[1, j], txh_r.at[1, j], x_prev))

    def recv_xh(j):
        far = ring(x, 2)
        recv(T.at[far, unit[j], pl.ds(0, half)], txh_r.at[0, j])
        recv(T.at[far, unit[j], pl.ds(half, half)], txh_r.at[1, j])

    quarter = 128

    def send_c(u, r):
        block = W.at[ring(y, r), wunit[u], c]
        go(remote(block, block, wc_s.at[u, r % 4], wc_r.at[u, r % 4], sibling))

    def send_y(u):
        block = W.at[y, wunit[u], c]
        for side, to in enumerate((y_next, y_prev)):
            go(remote(block, block, wy_s.at[side, u], wy_r.at[side, u], to))
        send_c(u, 0)

    def recv_y(u):
        left, right = ring(y, -1), ring(y, 1)
        recv(W.at[left, wunit[u], c], wy_r.at[0, u])
        block = W.at[left, wunit[u], c, pl.ds(0, quarter)]
        go(remote(block, block, wyh_s.at[0, u], wyh_r.at[0, u], y_next))
        send_c(u, -1)
        recv(W.at[right, wunit[u], c], wy_r.at[1, u])
        block = W.at[right, wunit[u], c, pl.ds(quarter, quarter)]
        go(remote(block, block, wyh_s.at[1, u], wyh_r.at[1, u], y_prev))
        send_c(u, 1)

    def recv_yh(u):
        far = ring(y, 2)
        recv(W.at[far, wunit[u], c, pl.ds(0, quarter)], wyh_r.at[0, u])
        recv(W.at[far, wunit[u], c, pl.ds(quarter, quarter)], wyh_r.at[1, u])
        send_c(u, 2)

    def recv_c(u):
        for r in range(4):
            recv(W.at[ring(y, r), wunit[u], 1 - c], wc_r.at[u, r])

    def send_wz():
        block = W.at[y, zh, c]
        for side, to in enumerate((h_next, h_prev)):
            go(remote(block, block, wz_s.at[side], wz_r.at[side], to))

    def recv_wz():
        left, right = wunit[1], wunit[2]
        recv(W.at[y, left, c], wz_r.at[0])
        block = W.at[y, left, c, pl.ds(0, quarter)]
        go(remote(block, block, wzh_s.at[0], wzh_r.at[0], h_next))
        send_y(1)
        recv(W.at[y, right, c], wz_r.at[1])
        block = W.at[y, right, c, pl.ds(quarter, quarter)]
        go(remote(block, block, wzh_s.at[1], wzh_r.at[1], h_prev))
        send_y(2)

    def recv_wzh():
        recv(W.at[y, wunit[3], c, pl.ds(0, quarter)], wzh_r.at[0])
        recv(W.at[y, wunit[3], c, pl.ds(quarter, quarter)], wzh_r.at[1])
        send_y(3)

    def sum_send(buf, me, s, r, to):
        for d in range(1, len(to) + 1):
            go(remote(buf.at[me], buf.at[me], s.at[d - 1], r.at[me], to[d - 1]))

    def sum_recv(buf, me, r, n):
        for d in range(1, n):
            other = (me + d) % n
            recv(buf.at[other], r.at[other])
        total = buf[0] + buf[1]
        for i in range(2, n):
            total = total + buf[i]
        return total

    send_x(0)
    send_z(0)
    send_y(0)
    if WEIGHT_START == 0:
        send_wz()
    for load in loads[2:]:
        load.wait()

    @pl.when(off_diagonal)
    def _():
        recv(down_t.at[c], dt_r.at[c])

    recv(down_t.at[1 - c], dt_r.at[1 - c])
    tok = T[x, zl]
    down_columns = jnp.concatenate([down_t[0], down_t[1]], axis=1).astype(jnp.bfloat16)
    arx[x, 0:8] = dot(down_columns, tok, ((1,), (1,)))
    arx[x, 8:16] = dot(up[...], cot[...], ((1,), (1,)))
    sum_send(arx, x, arx_s, arx_r, [dev(x=ring(x, d)) for d in (1, 2, 3)])

    recv_y(0)
    recv_z(1)
    recv_x(0)

    arz[zl] = sum_recv(arx, x, arx_r, 4)
    sum_send(arz, zl, arz_s, arz_r, [dev(zl=ring(zl, d)) for d in (1, 2, 3)])
    if WEIGHT_START == 1:
        send_wz()
    recv_z(2)
    if WEIGHT_START == 2:
        send_wz()
    recv_yh(0)

    both = sum_recv(arz, zl, arz_r, 4)
    low, back = both[0:8].astype(jnp.bfloat16), both[8:16].astype(jnp.bfloat16)
    arc[c, 0:8] = adapter_scale * dot(low, cot[...], ((1,), (0,)))
    arc[c, 8:16] = adapter_scale * dot(back, T[x, zl], ((1,), (0,)))
    sum_send(arc, c, arc_s, arc_r, [sibling])
    acc[...] = adapter_scale * dot(low, up[...], ((0,), (0,)))

    recv_x(1)
    ary[y] = sum_recv(arc, c, arc_r, 2)
    sum_send(ary, y, ary_s, ary_r, [dev(y=ring(y, d)) for d in (1, 2, 3)])
    recv_z(3)
    if WEIGHT_START == 3:
        send_wz()
    recv_xh(0)
    recv_c(0)

    def products(stage):
        for u in range(4):
            here = 0
            for j in range(4):
                here = here + jnp.where(unit[j] == wunit[u], j, 0)

            @pl.when(jnp.maximum(here, u) == stage)
            def _(u=u):
                @pl.loop(0, 4)
                def _(i):
                    weights = W[i, wunit[u]].reshape(512, 512)
                    for r in range(2):
                        rows = pl.ds(r * 256, 256)
                        acc[rows] += dot(T[i, wunit[u], rows], weights, ((1,), (0,)))

    products(0)
    arh[zh] = sum_recv(ary, y, ary_r, 4)
    sum_send(arh, zh, arh_s, arh_r, [dev(zh=ring(zh, d)) for d in (1, 2, 3)])
    recv_x(2)
    recv_wz()
    recv_xh(1)

    grads = sum_recv(arh, zh, arh_r, 4)
    upg[...] = grads[0:8]
    dtot[0] = grads[8:16, 0:256]
    dtot[1] = grads[8:16, 256:512]
    gradient_mirror = remote(dtot.at[c], dng, dg_s, dg_r, mirror(c))

    @pl.when(off_diagonal)
    def _():
        gradient_mirror.start()

    @pl.when(jnp.logical_not(off_diagonal))
    def _():
        dng[...] = dtot[c]

    recv_y(1)
    recv_y(2)
    recv_wzh()
    recv_x(3)

    @pl.when(off_diagonal)
    def _():
        gradient_mirror.wait_recv()

    stores = [
        pltpu.make_async_copy(src, dst, store_sem.at[i])
        for i, (src, dst) in enumerate(
            [(upg, upg_out), (dng, dng_out), (newimp, newimp_out), (proj, proj_out)]
        )
    ]
    stores[0].start()
    stores[1].start()
    highest = lax.Precision.HIGHEST
    own_down = down[...]
    estimate = dot(dng[...], up[...].astype(jnp.float32), ((0,), (0,)), highest)
    estimate = estimate + dot(own_down.astype(jnp.float32), upg[...], ((0,), (0,)), highest)
    merged = W[y, zh, c].astype(jnp.float32) + adapter_scale * dot(own_down, up[...], ((0,), (0,)))
    newimp[...] = decay_rate * imp[...] + (1.0 - decay_rate) * jnp.abs(merged * estimate)
    stores[2].start()

    recv_yh(1)
    recv_yh(2)
    recv_c(1)
    products(1)
    recv_y(3)
    recv_xh(2)
    recv_yh(3)
    recv_c(2)
    products(2)
    recv_c(3)
    recv_xh(3)
    products(3)
    proj[...] = acc[...].astype(jnp.bfloat16)
    stores[3].start()

    for copy in sends:
        copy.wait_send()
    for cond, copy in z_forwards:

        @pl.when(cond)
        def _(copy=copy):
            copy.wait_send()

    @pl.when(jnp.logical_not(off_diagonal))
    def _():
        down_away.wait_send()

    @pl.when(off_diagonal)
    def _():
        for copy in down_mirror:
            copy.wait_send()
        gradient_mirror.wait_send()

    for store in stores:
        store.wait()


def local(tokens, weight, down, up, cotangent, importance):
    bf16, f32 = jnp.bfloat16, jnp.float32
    dma = pltpu.SemaphoreType.DMA
    return pl.pallas_call(
        kernel,
        out_shape=(
            jax.ShapeDtypeStruct((512, 512), bf16),
            jax.ShapeDtypeStruct((8, 512), f32),
            jax.ShapeDtypeStruct((8, 256), f32),
            jax.ShapeDtypeStruct((256, 512), f32),
        ),
        in_specs=[
            pl.BlockSpec(memory_space=pltpu.VMEM if i in (2, 3) else pl.ANY) for i in range(6)
        ],
        out_specs=[pl.BlockSpec(memory_space=pl.ANY)] * 4,
        scratch_shapes=[
            pltpu.VMEM((4, 4, 512, 512), bf16),
            pltpu.VMEM((4, 4, 2, 256, 512), bf16),
            pltpu.VMEM((512, 512), f32),
            pltpu.VMEM((512, 512), bf16),
            pltpu.VMEM((512, 512), bf16),
            pltpu.VMEM((256, 512), f32),
            pltpu.VMEM((256, 512), f32),
            pltpu.VMEM((8, 512), f32),
            pltpu.VMEM((8, 256), f32),
            pltpu.VMEM((2, 8, 256), f32),
            pltpu.VMEM((3, 8, 256), f32),
            pltpu.VMEM((4, 16, 512), f32),
            pltpu.VMEM((4, 16, 512), f32),
            pltpu.VMEM((2, 16, 512), f32),
            pltpu.VMEM((4, 16, 512), f32),
            pltpu.VMEM((4, 16, 512), f32),
            dma((4,)), dma((4,)),
            dma((2, 4)), dma((2, 4)), dma((2, 4)), dma((2, 4)), dma((2, 4)), dma((4,)),
            dma((2,)), dma((2,)), dma((2,)), dma((2,)),
            dma((2, 4)), dma((2, 4)), dma((2, 4)), dma((2, 4)), dma((4, 4)), dma((4, 4)),
            dma((3,)), dma((4,)), dma((3,)), dma((4,)), dma((1,)), dma((2,)),
            dma((3,)), dma((4,)), dma((3,)), dma((4,)),
            dma((3,)), dma((2,)), dma, dma,
        ],
        compiler_params=pltpu.CompilerParams(
            collective_id=0, has_side_effects=True, vmem_limit_bytes=48 * 2**20
        ),
    )(tokens, weight, down, up, cotangent, importance)


def solution(mesh):
    placed = (
        P("fsdp", "tp"),
        P("fsdp", "tp"),
        P(None, "fsdp"),
        P(None, "tp"),
        P("fsdp", "tp"),
        P("fsdp", "tp"),
    )
    return jax.shard_map(
        local,
        mesh=mesh,
        in_specs=placed,
        out_specs=(P("fsdp", "tp"), P(None, "tp"), P(None, "fsdp"), P("fsdp", "tp")),
        check_vma=False,
    )
```

```python
import jax
import jax.numpy as jnp
from jax import lax
from jax.experimental import pallas as pl
from jax.experimental.pallas import tpu as pltpu
from jax.sharding import PartitionSpec as P

adapter_scale = 2.0
decay_rate = 0.8
MESH = pl.DeviceIdType.MESH


def dot(a, b, dims, precision=None):
    return lax.dot_general(
        a, b, (dims, ((), ())), preferred_element_type=jnp.float32, precision=precision
    )


def kernel(
    tok_in, w_in, down, up, cot_in, imp_in,
    proj_out, upg_out, dng_out, newimp_out,
    T, W, acc, proj, cot, imp, newimp, upg, dng, down_t, dtot,
    arx, arz, arc, ary, arh,
    load_sem, store_sem,
    tx_s, tx_r, txh_s, txh_r, tz_s, tz_r,
    wz_s, wz_r, wzh_s, wzh_r, wy_s, wy_r, wyh_s, wyh_r, wc_s, wc_r,
    arx_s, arx_r, arz_s, arz_r, arc_s, arc_r, ary_s, ary_r, arh_s, arh_r,
    dt_s, dt_r, dg_s, dg_r,
):
    f = lax.axis_index("fsdp")
    t = lax.axis_index("tp")
    chip = f // 2
    c = f % 2
    y, zh = chip // 4, chip % 4
    x, zl = t // 4, t % 4

    def dev(y=y, zh=zh, c=c, x=x, zl=zl):
        return {"fsdp": (y * 4 + zh) * 2 + c, "tp": x * 4 + zl}

    def ring(i, d):
        return (i + d + 4) % 4

    x_next, x_prev = dev(x=ring(x, 1)), dev(x=ring(x, -1))
    y_next, y_prev = dev(y=ring(y, 1)), dev(y=ring(y, -1))
    h_next, h_prev = dev(zh=ring(zh, 1)), dev(zh=ring(zh, -1))
    l_next, l_prev = dev(zl=ring(zl, 1)), dev(zl=ring(zl, -1))
    sibling = dev(c=1 - c)
    off_diagonal = chip != t

    def mirror(core):
        return {"fsdp": t * 2 + core, "tp": chip}

    def remote(src, dst, send, recv, to):
        return pltpu.make_async_remote_copy(
            src_ref=src, dst_ref=dst, send_sem=send, recv_sem=recv, device_id=to, device_id_type=MESH
        )

    loads = [
        pltpu.make_async_copy(src, dst, load_sem.at[i])
        for i, (src, dst) in enumerate(
            [
                (tok_in, T.at[x, zl]),
                (w_in, W.at[y, zh, c]),
                (cot_in, cot),
                (imp_in, imp),
            ]
        )
    ]
    for load in loads:
        load.start()

    barrier = pltpu.get_barrier_semaphore()
    for r in (1, 2, 3):
        for partner in (dev(x=ring(x, r)), dev(y=ring(y, r)), dev(zh=ring(zh, r)), dev(zl=ring(zl, r))):
            pl.semaphore_signal(barrier, inc=1, device_id=partner, device_id_type=MESH)
    pl.semaphore_signal(barrier, inc=1, device_id=sibling, device_id_type=MESH)

    @pl.when(off_diagonal)
    def _():
        for core in (0, 1):
            pl.semaphore_signal(barrier, inc=1, device_id=mirror(core), device_id_type=MESH)

    for load in loads[:2]:
        load.wait()
    down_f32 = down[...].astype(jnp.float32)
    dtot[2] = down_f32
    pl.semaphore_wait(barrier, jnp.where(off_diagonal, 15, 13))

    sends = []

    def go(copy):
        copy.start()
        sends.append(copy)
        return copy

    down_away = remote(dtot.at[2], down_t.at[c], dt_s.at[0], dt_r.at[c], sibling)
    down_mirror = [
        remote(dtot.at[2], down_t.at[c], dt_s.at[1 + core], dt_r.at[c], mirror(core)) for core in (0, 1)
    ]

    @pl.when(jnp.logical_not(off_diagonal))
    def _():
        down_t[c] = down_f32
        down_away.start()

    @pl.when(off_diagonal)
    def _():
        for copy in down_mirror:
            copy.start()

    unit = [
        zl,
        jnp.where(zl == 0, 1, jnp.where(zl == 1, 0, jnp.where(zl == 2, 1, 2))),
        jnp.where(zl == 0, 2, jnp.where(zl == 1, 2, jnp.where(zl == 2, 3, 1))),
        jnp.where(zl < 2, 3, 0),
    ]
    wunit = [zh, ring(zh, -1), ring(zh, 1), ring(zh, 2)]

    half, quarter = 256, 128

    def rows(h, size):
        return pl.ds(h * size, size)

    def recv(dst, sem):
        remote(dst, dst, sem, sem, sibling).wait_recv()

    def send_x(j, h):
        block = T.at[x, unit[j], rows(h, half)]
        for side, to in enumerate((x_next, x_prev)):
            go(remote(block, block, tx_s.at[side, j, h], tx_r.at[side, j, h], to))

    def send_x0(k):
        for side, to in enumerate((x_next, x_prev)):
            h = k if side == 0 else 1 - k
            block = T.at[x, zl, rows(h, half)]
            go(remote(block, block, tx_s.at[side, 0, h], tx_r.at[side, 0, h], to))

    z_forwards = []

    def send_z(j, h):
        block = T.at[x, unit[j], rows(h, half)]
        if j == 0:
            cases = ((zl < 3, l_next, 0), (zl > 0, l_prev, 1))
        else:
            cases = (
                (jnp.logical_and(unit[j] < zl, zl < 3), l_next, 0),
                (jnp.logical_and(unit[j] > zl, zl > 0), l_prev, 1),
            )
        for cond, to, side in cases:
            copy = remote(block, block, tz_s.at[side, j, h], tz_r.at[unit[j], h], to)
            z_forwards.append((cond, copy))

            @pl.when(cond)
            def _(copy=copy):
                copy.start()

    def recv_z(j, h):
        recv(T.at[x, unit[j], rows(h, half)], tz_r.at[unit[j], h])
        send_z(j, h)
        send_x(j, h)

    def forward_x(j, h):
        near, to = (ring(x, -1), x_next) if h == 0 else (ring(x, 1), x_prev)
        block = T.at[near, unit[j], rows(h, half)]
        recv(block, tx_r.at[h, j, h])
        go(remote(block, block, txh_s.at[h, j], txh_r.at[h, j], to))

    def rest_x(j):
        recv(T.at[ring(x, -1), unit[j], rows(1, half)], tx_r.at[0, j, 1])
        recv(T.at[ring(x, 1), unit[j], rows(0, half)], tx_r.at[1, j, 0])

    def far_x(j):
        for h in (0, 1):
            recv(T.at[ring(x, 2), unit[j], rows(h, half)], txh_r.at[h, j])

    def send_c(u, r):
        block = W.at[ring(y, r), wunit[u], c]
        go(remote(block, block, wc_s.at[u, r % 4], wc_r.at[u, r % 4], sibling))

    def send_y(u, h):
        block = W.at[y, wunit[u], c, rows(h, quarter)]
        for side, to in enumerate((y_next, y_prev)):
            go(remote(block, block, wy_s.at[side, u, h], wy_r.at[side, u, h], to))

    def forward_y(u, h):
        near, to = (ring(y, -1), y_next) if h == 0 else (ring(y, 1), y_prev)
        block = W.at[near, wunit[u], c, rows(h, quarter)]
        recv(block, wy_r.at[h, u, h])
        go(remote(block, block, wyh_s.at[h, u], wyh_r.at[h, u], to))

    def rest_y(u):
        recv(W.at[ring(y, -1), wunit[u], c, rows(1, quarter)], wy_r.at[0, u, 1])
        send_c(u, -1)
        recv(W.at[ring(y, 1), wunit[u], c, rows(0, quarter)], wy_r.at[1, u, 0])
        send_c(u, 1)

    def far_y(u):
        for h in (0, 1):
            recv(W.at[ring(y, 2), wunit[u], c, rows(h, quarter)], wyh_r.at[h, u])
        send_c(u, 2)

    def recv_c(u):
        for r in range(4):
            recv(W.at[ring(y, r), wunit[u], 1 - c], wc_r.at[u, r])

    def send_wz(k):
        for side, to in enumerate((h_next, h_prev)):
            h = k if side == 0 else 1 - k
            block = W.at[y, zh, c, rows(h, quarter)]
            go(remote(block, block, wz_s.at[side, h], wz_r.at[side, h], to))

    def forward_wz(h):
        near, to = (wunit[1], h_next) if h == 0 else (wunit[2], h_prev)
        block = W.at[y, near, c, rows(h, quarter)]
        recv(block, wz_r.at[h, h])
        go(remote(block, block, wzh_s.at[h], wzh_r.at[h], to))
        send_y(1 + h, h)

    def rest_wz():
        recv(W.at[y, wunit[1], c, rows(1, quarter)], wz_r.at[0, 1])
        send_y(1, 1)
        send_c(1, 0)
        recv(W.at[y, wunit[2], c, rows(0, quarter)], wz_r.at[1, 0])
        send_y(2, 0)
        send_c(2, 0)

    def far_wz():
        for h in (0, 1):
            recv(W.at[y, wunit[3], c, rows(h, quarter)], wzh_r.at[h])
            send_y(3, h)
        send_c(3, 0)

    def sum_send(buf, me, s, r, to):
        for d in range(1, len(to) + 1):
            go(remote(buf.at[me], buf.at[me], s.at[d - 1], r.at[me], to[d - 1]))

    def sum_recv(buf, me, r, n):
        for d in range(1, n):
            other = (me + d) % n
            recv(buf.at[other], r.at[other])
        total = buf[0] + buf[1]
        for i in range(2, n):
            total = total + buf[i]
        return total

    send_x0(0)
    for h in (0, 1):
        send_z(0, h)
        send_y(0, h)
    send_c(0, 0)
    for load in loads[2:]:
        load.wait()

    @pl.when(off_diagonal)
    def _():
        recv(down_t.at[c], dt_r.at[c])

    recv(down_t.at[1 - c], dt_r.at[1 - c])
    down_columns = jnp.concatenate([down_t[0], down_t[1]], axis=1).astype(jnp.bfloat16)
    arx[x, 0:8] = dot(down_columns, T[x, zl], ((1,), (1,)))
    arx[x, 8:16] = dot(up[...], cot[...], ((1,), (1,)))
    sum_send(arx, x, arx_s, arx_r, [dev(x=ring(x, d)) for d in (1, 2, 3)])
    send_x0(1)

    def sum_low():
        arz[zl] = sum_recv(arx, x, arx_r, 4)
        sum_send(arz, zl, arz_s, arz_r, [dev(zl=ring(zl, d)) for d in (1, 2, 3)])

    def factor_terms():
        both = sum_recv(arz, zl, arz_r, 4)
        low, back = both[0:8].astype(jnp.bfloat16), both[8:16].astype(jnp.bfloat16)
        arc[c, 0:8] = adapter_scale * dot(low, cot[...], ((1,), (0,)))
        arc[c, 8:16] = adapter_scale * dot(back, T[x, zl], ((1,), (0,)))
        sum_send(arc, c, arc_s, arc_r, [sibling])
        acc[...] = adapter_scale * dot(low, up[...], ((0,), (0,)))

    def sum_cores():
        ary[y] = sum_recv(arc, c, arc_r, 2)
        sum_send(ary, y, ary_s, ary_r, [dev(y=ring(y, d)) for d in (1, 2, 3)])

    def sum_y():
        arh[zh] = sum_recv(ary, y, ary_r, 4)
        sum_send(arh, zh, arh_s, arh_r, [dev(zh=ring(zh, d)) for d in (1, 2, 3)])

    def gradient_copy():
        return remote(dtot.at[c], dng, dg_s, dg_r, mirror(c))

    def sum_gradients():
        grads = sum_recv(arh, zh, arh_r, 4)
        upg[...] = grads[0:8]
        dtot[0] = grads[8:16, 0:256]
        dtot[1] = grads[8:16, 256:512]

        @pl.when(off_diagonal)
        def _():
            gradient_copy().start()

        @pl.when(jnp.logical_not(off_diagonal))
        def _():
            dng[...] = dtot[c]

    stores = [
        pltpu.make_async_copy(src, dst, store_sem.at[i])
        for i, (src, dst) in enumerate(
            [(upg, upg_out), (dng, dng_out), (newimp, newimp_out), (proj, proj_out)]
        )
    ]

    def importance():
        @pl.when(off_diagonal)
        def _():
            gradient_copy().wait_recv()

        stores[0].start()
        stores[1].start()
        highest = lax.Precision.HIGHEST
        own_down = down[...]
        estimate = dot(dng[...], up[...].astype(jnp.float32), ((0,), (0,)), highest)
        estimate = estimate + dot(own_down.astype(jnp.float32), upg[...], ((0,), (0,)), highest)
        merged = W[y, zh, c].astype(jnp.float32) + adapter_scale * dot(own_down, up[...], ((0,), (0,)))
        newimp[...] = decay_rate * imp[...] + (1.0 - decay_rate) * jnp.abs(merged * estimate)
        stores[2].start()

    def products(stage):
        for u in range(4):
            here = 0
            for j in range(4):
                here = here + jnp.where(unit[j] == wunit[u], j, 0)

            @pl.when(jnp.maximum(here, u) == stage)
            def _(u=u):
                @pl.loop(0, 4)
                def _(i):
                    weights = W[i, wunit[u]].reshape(512, 512)
                    for r in range(2):
                        chunk = pl.ds(r * 256, 256)
                        acc[chunk] += dot(T[i, wunit[u], chunk], weights, ((1,), (0,)))

    recv_z(1, 0)
    sum_low()
    recv_z(1, 1)
    send_wz(0)
    forward_x(0, 0)
    forward_x(0, 1)
    forward_y(0, 0)
    forward_y(0, 1)
    recv_z(2, 0)
    recv_z(2, 1)
    send_wz(1)
    factor_terms()
    forward_x(1, 0)
    forward_x(1, 1)
    sum_cores()
    rest_y(0)
    far_y(0)
    recv_z(3, 0)
    recv_z(3, 1)
    forward_wz(0)
    forward_wz(1)
    forward_x(2, 0)
    forward_x(2, 1)
    sum_y()
    rest_x(0)
    far_x(0)
    recv_c(0)
    rest_wz()
    forward_y(1, 0)
    forward_y(2, 1)
    rest_x(1)
    far_x(1)
    forward_x(3, 0)
    forward_x(3, 1)
    far_wz()
    sum_gradients()
    forward_y(1, 1)
    forward_y(2, 0)
    forward_y(3, 0)
    forward_y(3, 1)
    rest_y(1)
    rest_y(2)
    importance()
    far_y(1)
    far_y(2)
    rest_x(2)
    far_x(2)
    recv_c(1)
    recv_c(2)
    rest_y(3)
    far_y(3)
    recv_c(3)
    products(0)
    products(1)
    products(2)
    rest_x(3)
    far_x(3)
    products(3)
    proj[...] = acc[...].astype(jnp.bfloat16)
    stores[3].start()

    for copy in sends:
        copy.wait_send()
    for cond, copy in z_forwards:

        @pl.when(cond)
        def _(copy=copy):
            copy.wait_send()

    @pl.when(jnp.logical_not(off_diagonal))
    def _():
        down_away.wait_send()

    @pl.when(off_diagonal)
    def _():
        for copy in down_mirror:
            copy.wait_send()
        gradient_copy().wait_send()

    for store in stores:
        store.wait()


def local(tokens, weight, down, up, cotangent, importance):
    bf16, f32 = jnp.bfloat16, jnp.float32
    dma = pltpu.SemaphoreType.DMA
    return pl.pallas_call(
        kernel,
        out_shape=(
            jax.ShapeDtypeStruct((512, 512), bf16),
            jax.ShapeDtypeStruct((8, 512), f32),
            jax.ShapeDtypeStruct((8, 256), f32),
            jax.ShapeDtypeStruct((256, 512), f32),
        ),
        in_specs=[
            pl.BlockSpec(memory_space=pltpu.VMEM if i in (2, 3) else pltpu.HBM) for i in range(6)
        ],
        out_specs=[pl.BlockSpec(memory_space=pl.ANY)] * 4,
        scratch_shapes=[
            pltpu.VMEM((4, 4, 512, 512), bf16),
            pltpu.VMEM((4, 4, 2, 256, 512), bf16),
            pltpu.VMEM((512, 512), f32),
            pltpu.VMEM((512, 512), bf16),
            pltpu.VMEM((512, 512), bf16),
            pltpu.VMEM((256, 512), f32),
            pltpu.VMEM((256, 512), f32),
            pltpu.VMEM((8, 512), f32),
            pltpu.VMEM((8, 256), f32),
            pltpu.VMEM((2, 8, 256), f32),
            pltpu.VMEM((3, 8, 256), f32),
            pltpu.VMEM((4, 16, 512), f32),
            pltpu.VMEM((4, 16, 512), f32),
            pltpu.VMEM((2, 16, 512), f32),
            pltpu.VMEM((4, 16, 512), f32),
            pltpu.VMEM((4, 16, 512), f32),
            dma((4,)), dma((4,)),
            dma((2, 4, 2)), dma((2, 4, 2)), dma((2, 4)), dma((2, 4)), dma((2, 4, 2)), dma((4, 2)),
            dma((2, 2)), dma((2, 2)), dma((2,)), dma((2,)),
            dma((2, 4, 2)), dma((2, 4, 2)), dma((2, 4)), dma((2, 4)), dma((4, 4)), dma((4, 4)),
            dma((3,)), dma((4,)), dma((3,)), dma((4,)), dma((1,)), dma((2,)),
            dma((3,)), dma((4,)), dma((3,)), dma((4,)),
            dma((3,)), dma((2,)), dma, dma,
        ],
        compiler_params=pltpu.CompilerParams(
            collective_id=0, has_side_effects=True, vmem_limit_bytes=63 * 2**20
        ),
    )(tokens, weight, down, up, cotangent, importance)


def solution(mesh):
    placed = (
        P("fsdp", "tp"),
        P("fsdp", "tp"),
        P(None, "fsdp"),
        P(None, "tp"),
        P("fsdp", "tp"),
        P("fsdp", "tp"),
    )
    return jax.shard_map(
        local,
        mesh=mesh,
        in_specs=placed,
        out_specs=(P("fsdp", "tp"), P(None, "tp"), P(None, "fsdp"), P("fsdp", "tp")),
        check_vma=False,
    )
```

```python
import jax
import jax.numpy as jnp
from jax import lax
from jax.experimental import pallas as pl
from jax.experimental.pallas import tpu as pltpu
from jax.sharding import PartitionSpec as P

adapter_scale = 2.0
decay_rate = 0.8
MESH = pl.DeviceIdType.MESH


def dot(a, b, dims, precision=None):
    return lax.dot_general(
        a, b, (dims, ((), ())), preferred_element_type=jnp.float32, precision=precision
    )


def kernel(
    tok_in, w_in, down, up, cot_in, imp_in,
    proj_out, upg_out, dng_out, newimp_out,
    T, W, acc, proj, cot, imp, newimp, upg, dng, down_t, dtot,
    arx, arz, arc, ary, arh,
    load_sem, store_sem,
    tx_s, tx_r, txh_s, txh_r, tz_s, tz_r,
    wz_s, wz_r, wzh_s, wzh_r, wy_s, wy_r, wyh_s, wyh_r, wc_s, wc_r,
    arx_s, arx_r, arz_s, arz_r, arc_s, arc_r, ary_s, ary_r, arh_s, arh_r,
    dt_s, dt_r, dg_s, dg_r,
):
    f = lax.axis_index("fsdp")
    t = lax.axis_index("tp")
    chip = f // 2
    c = f % 2
    y, zh = chip // 4, chip % 4
    x, zl = t // 4, t % 4

    def dev(y=y, zh=zh, c=c, x=x, zl=zl):
        return {"fsdp": (y * 4 + zh) * 2 + c, "tp": x * 4 + zl}

    def ring(i, d):
        return (i + d + 4) % 4

    x_next, x_prev = dev(x=ring(x, 1)), dev(x=ring(x, -1))
    y_next, y_prev = dev(y=ring(y, 1)), dev(y=ring(y, -1))
    h_next, h_prev = dev(zh=ring(zh, 1)), dev(zh=ring(zh, -1))
    l_next, l_prev = dev(zl=ring(zl, 1)), dev(zl=ring(zl, -1))
    sibling = dev(c=1 - c)
    off_diagonal = chip != t

    def mirror(core):
        return {"fsdp": t * 2 + core, "tp": chip}

    def remote(src, dst, send, recv, to):
        return pltpu.make_async_remote_copy(
            src_ref=src, dst_ref=dst, send_sem=send, recv_sem=recv, device_id=to, device_id_type=MESH
        )

    loads = [
        pltpu.make_async_copy(src, dst, load_sem.at[i])
        for i, (src, dst) in enumerate(
            [
                (tok_in, T.at[x, zl]),
                (w_in, W.at[y, zh, c]),
                (cot_in, cot),
                (imp_in, imp),
            ]
        )
    ]
    for load in loads:
        load.start()

    barrier = pltpu.get_barrier_semaphore()
    for r in (1, 2, 3):
        for partner in (dev(x=ring(x, r)), dev(y=ring(y, r)), dev(zh=ring(zh, r)), dev(zl=ring(zl, r))):
            pl.semaphore_signal(barrier, inc=1, device_id=partner, device_id_type=MESH)
    pl.semaphore_signal(barrier, inc=1, device_id=sibling, device_id_type=MESH)

    @pl.when(off_diagonal)
    def _():
        for core in (0, 1):
            pl.semaphore_signal(barrier, inc=1, device_id=mirror(core), device_id_type=MESH)

    for load in loads[:2]:
        load.wait()
    down_f32 = down[...].astype(jnp.float32)
    dtot[2] = down_f32
    pl.semaphore_wait(barrier, jnp.where(off_diagonal, 15, 13))

    sends = []

    def go(copy):
        copy.start()
        sends.append(copy)
        return copy

    def go_later(copy):
        sends.append(copy)
        return copy

    down_away = remote(dtot.at[2], down_t.at[c], dt_s.at[0], dt_r.at[c], sibling)
    down_mirror = [
        remote(dtot.at[2], down_t.at[c], dt_s.at[1 + core], dt_r.at[c], mirror(core)) for core in (0, 1)
    ]

    @pl.when(jnp.logical_not(off_diagonal))
    def _():
        down_t[c] = down_f32
        down_away.start()

    @pl.when(off_diagonal)
    def _():
        for copy in down_mirror:
            copy.start()

    unit = [
        zl,
        jnp.where(zl == 0, 1, jnp.where(zl == 1, 0, jnp.where(zl == 2, 1, 2))),
        jnp.where(zl == 0, 2, jnp.where(zl == 1, 2, jnp.where(zl == 2, 3, 1))),
        jnp.where(zl < 2, 3, 0),
    ]
    wunit = [zh, ring(zh, -1), ring(zh, 1), ring(zh, 2)]

    def rows(p, size):
        return pl.ds(p * size, size)

    def recv(dst, sem):
        remote(dst, dst, sem, sem, sibling).wait_recv()

    tp, wp = 128, 64

    def send_x(j, p, sides=(0, 1)):
        block = T.at[x, unit[j], rows(p, tp)]
        for side in sides:
            to = (x_next, x_prev)[side]
            go(remote(block, block, tx_s.at[side, j, p], tx_r.at[side, j, p], to))

    z_forwards = []
    z_last = []

    def send_z(j, p):
        block = T.at[x, unit[j], rows(p, tp)]
        if j == 0:
            cases = ((zl < 3, l_next, 0), (zl > 0, l_prev, 1))
        else:
            cases = (
                (jnp.logical_and(unit[j] < zl, zl < 3), l_next, 0),
                (jnp.logical_and(unit[j] > zl, zl > 0), l_prev, 1),
            )
        for cond, to, side in cases:
            copy = remote(block, block, tz_s.at[side, j, p], tz_r.at[unit[j], p], to)
            z_forwards.append((cond, copy))

            @pl.when(cond)
            def _(copy=copy):
                copy.start()

    def recv_z(j, p):
        recv(T.at[x, unit[j], rows(p, tp)], tz_r.at[unit[j], p])
        send_z(j, p)
        send_x(j, p)

    middle = jnp.logical_and(zl > 0, zl < 3)
    last_x = {}

    def recv_z_last(p, here):
        block = T.at[x, unit[3], rows(p, tp)]
        first = p not in last_x
        if first:
            last_x[p] = [
                go_later(remote(block, block, tx_s.at[side, 3, p], tx_r.at[side, 3, p], to))
                for side, to in enumerate((x_next, x_prev))
            ]
            for cond, to, side in (
                (jnp.logical_and(unit[3] < zl, zl < 3), l_next, 0),
                (jnp.logical_and(unit[3] > zl, zl > 0), l_prev, 1),
            ):
                copy = remote(block, block, tz_s.at[side, 3, p], tz_r.at[unit[3], p], to)
                z_forwards.append((cond, copy))
                z_last.append((p, cond, copy))

        @pl.when(here)
        def _():
            recv(block, tz_r.at[unit[3], p])
            for q, cond, copy in z_last:
                if q == p and first:
                    pl.when(cond)(copy.start)
            for copy in last_x[p]:
                copy.start()

    def forward_x(j, p):
        side = p // 2
        near, to = (ring(x, -1), x_next) if side == 0 else (ring(x, 1), x_prev)
        block = T.at[near, unit[j], rows(p, tp)]
        recv(block, tx_r.at[side, j, p])
        go(remote(block, block, txh_s.at[j, p], txh_r.at[j, p], to))

    def rest_x(j):
        for p in (2, 3):
            recv(T.at[ring(x, -1), unit[j], rows(p, tp)], tx_r.at[0, j, p])
        for p in (0, 1):
            recv(T.at[ring(x, 1), unit[j], rows(p, tp)], tx_r.at[1, j, p])

    def far_x(j):
        for p in range(4):
            recv(T.at[ring(x, 2), unit[j], rows(p, tp)], txh_r.at[j, p])

    def core_parts(u):
        return (pl.ds(0, 128), pl.ds(128, 128)) if u == 3 else (pl.ds(0, 256),)

    def send_c(u, r, part=0):
        block = W.at[ring(y, r), wunit[u], c, core_parts(u)[part]]
        go(remote(block, block, wc_s.at[u, r % 4, part], wc_r.at[u, r % 4, part], sibling))

    def recv_c(u):
        for r in range(4):
            for part, where in enumerate(core_parts(u)):
                recv(W.at[ring(y, r), wunit[u], 1 - c, where], wc_r.at[u, r, part])

    def send_y(u, p, sides=(0, 1)):
        block = W.at[y, wunit[u], c, rows(p, wp)]
        for side in sides:
            to = (y_next, y_prev)[side]
            go(remote(block, block, wy_s.at[side, u, p], wy_r.at[side, u, p], to))

    def forward_y(u, p):
        side = p // 2
        near, to = (ring(y, -1), y_next) if side == 0 else (ring(y, 1), y_prev)
        block = W.at[near, wunit[u], c, rows(p, wp)]
        recv(block, wy_r.at[side, u, p])
        go(remote(block, block, wyh_s.at[u, p], wyh_r.at[u, p], to))
        if u == 3 and p % 2 == 1:
            send_c(u, -1 if side == 0 else 1, side)

    def rest_y(u):
        for p in (2, 3):
            recv(W.at[ring(y, -1), wunit[u], c, rows(p, wp)], wy_r.at[0, u, p])
        send_c(u, -1, len(core_parts(u)) - 1)
        for p in (0, 1):
            recv(W.at[ring(y, 1), wunit[u], c, rows(p, wp)], wy_r.at[1, u, p])
        send_c(u, 1)

    def far_y(u):
        for p in range(4):
            recv(W.at[ring(y, 2), wunit[u], c, rows(p, wp)], wyh_r.at[u, p])
            if u == 3 and p == 1:
                send_c(u, 2)
        send_c(u, 2, len(core_parts(u)) - 1)

    def send_wz(k):
        for q in (0, 1):
            for side, to in enumerate((h_next, h_prev)):
                p = 2 * (k if side == 0 else 1 - k) + q
                block = W.at[y, zh, c, rows(p, wp)]
                go(remote(block, block, wz_s.at[side, p], wz_r.at[side, p], to))

    def forward_wz(p):
        side = p // 2
        near, to = (wunit[1], h_next) if side == 0 else (wunit[2], h_prev)
        block = W.at[y, near, c, rows(p, wp)]
        recv(block, wz_r.at[side, p])
        go(remote(block, block, wzh_s.at[p], wzh_r.at[p], to))
        send_y(1 + side, p)

    def rest_wz(p):
        u = 1 if p >= 2 else 2
        recv(W.at[y, wunit[u], c, rows(p, wp)], wz_r.at[u - 1, p])
        send_y(u, p)
        if p % 2 == 1:
            send_c(u, 0)

    def far_wz(p):
        recv(W.at[y, wunit[3], c, rows(p, wp)], wzh_r.at[p])
        send_y(3, p, (p // 2,))
        if p % 2 == 1:
            send_c(3, 0, p // 2)

    def far_wz_back():
        for p in (0, 2, 1, 3):
            send_y(3, p, (1 - p // 2,))

    def sum_send(buf, me, s, r, to):
        for d in range(1, len(to) + 1):
            go(remote(buf.at[me], buf.at[me], s.at[d - 1], r.at[me], to[d - 1]))

    def sum_recv(buf, me, r, n):
        for d in range(1, n):
            other = (me + d) % n
            recv(buf.at[other], r.at[other])
        total = buf[0] + buf[1]
        for i in range(2, n):
            total = total + buf[i]
        return total

    for p in (0, 1):
        send_x(0, p, (0,))
        send_x(0, 2 + p, (1,))
    for p in (0, 2, 1, 3):
        send_z(0, p)
    for p in (0, 1):
        send_y(0, p, (0,))
        send_y(0, 2 + p, (1,))
    for p in (0, 1):
        send_y(0, 2 + p, (0,))
        send_y(0, p, (1,))
    send_c(0, 0)
    for load in loads[2:]:
        load.wait()

    @pl.when(off_diagonal)
    def _():
        recv(down_t.at[c], dt_r.at[c])

    recv(down_t.at[1 - c], dt_r.at[1 - c])
    down_columns = jnp.concatenate([down_t[0], down_t[1]], axis=1).astype(jnp.bfloat16)
    arx[x, 0:8] = dot(down_columns, T[x, zl], ((1,), (1,)))
    arx[x, 8:16] = dot(up[...], cot[...], ((1,), (1,)))
    sum_send(arx, x, arx_s, arx_r, [dev(x=ring(x, d)) for d in (1, 2, 3)])
    for p in (0, 1):
        send_x(0, 2 + p, (0,))
        send_x(0, p, (1,))

    def sum_low():
        arz[zl] = sum_recv(arx, x, arx_r, 4)
        sum_send(arz, zl, arz_s, arz_r, [dev(zl=ring(zl, d)) for d in (1, 2, 3)])

    def factor_terms():
        both = sum_recv(arz, zl, arz_r, 4)
        low, back = both[0:8].astype(jnp.bfloat16), both[8:16].astype(jnp.bfloat16)
        arc[c, 0:8] = adapter_scale * dot(low, cot[...], ((1,), (0,)))
        arc[c, 8:16] = adapter_scale * dot(back, T[x, zl], ((1,), (0,)))
        sum_send(arc, c, arc_s, arc_r, [sibling])
        acc[...] = adapter_scale * dot(low, up[...], ((0,), (0,)))

    def sum_cores():
        ary[y] = sum_recv(arc, c, arc_r, 2)
        sum_send(ary, y, ary_s, ary_r, [dev(y=ring(y, d)) for d in (1, 2, 3)])

    def sum_y():
        arh[zh] = sum_recv(ary, y, ary_r, 4)
        sum_send(arh, zh, arh_s, arh_r, [dev(zh=ring(zh, d)) for d in (1, 2, 3)])

    def gradient_copy():
        return remote(dtot.at[c], dng, dg_s, dg_r, mirror(c))

    def sum_gradients():
        grads = sum_recv(arh, zh, arh_r, 4)
        upg[...] = grads[0:8]
        dtot[0] = grads[8:16, 0:256]
        dtot[1] = grads[8:16, 256:512]

        @pl.when(off_diagonal)
        def _():
            gradient_copy().start()

        @pl.when(jnp.logical_not(off_diagonal))
        def _():
            dng[...] = dtot[c]

    stores = [
        pltpu.make_async_copy(src, dst, store_sem.at[i])
        for i, (src, dst) in enumerate(
            [(upg, upg_out), (dng, dng_out), (newimp, newimp_out), (proj, proj_out)]
        )
    ]

    def importance():
        @pl.when(off_diagonal)
        def _():
            gradient_copy().wait_recv()

        stores[0].start()
        stores[1].start()
        highest = lax.Precision.HIGHEST
        own_down = down[...]
        estimate = dot(dng[...], up[...].astype(jnp.float32), ((0,), (0,)), highest)
        estimate = estimate + dot(own_down.astype(jnp.float32), upg[...], ((0,), (0,)), highest)
        merged = W[y, zh, c].astype(jnp.float32) + adapter_scale * dot(own_down, up[...], ((0,), (0,)))
        newimp[...] = decay_rate * imp[...] + (1.0 - decay_rate) * jnp.abs(merged * estimate)
        stores[2].start()

    def product(u, j):
        @pl.when(unit[j] == wunit[u])
        def _():
            @pl.loop(0, 4)
            def _(i):
                weights = W[i, wunit[u]].reshape(512, 512)
                for r in range(2):
                    chunk = pl.ds(r * 256, 256)
                    acc[chunk] += dot(T[i, wunit[u], chunk], weights, ((1,), (0,)))

    recv_z(1, 0)
    sum_low()
    recv_z(1, 2)
    recv_z(1, 1)
    recv_z(1, 3)
    for p in (0, 2, 1, 3):
            forward_x(0, p)
    for p in (0, 2, 1, 3):
            recv_z(2, p)
    send_wz(0)
    for p in (0, 2):
            recv_z_last(p, middle)
    send_wz(1)
    for p in (0, 2, 1, 3):
            forward_y(0, p)
    factor_terms()
    for p in (0, 2, 1, 3):
            forward_x(1, p)
    sum_cores()
    rest_y(0)
    far_y(0)
    rest_x(0)
    far_x(0)
    recv_c(0)
    product(0, 0)
    for p in (0, 2, 1, 3):
            forward_wz(p)
    for p in (1, 3):
            recv_z_last(p, middle)
    for p in (0, 2, 1, 3):
            forward_x(2, p)
    for p in (0, 2):
            recv_z_last(p, jnp.logical_not(middle))
    sum_y()
    for p in (0, 2, 1, 3):
            rest_wz(p)
    for u, p in ((1, 0), (2, 2), (1, 1), (2, 3)):
            forward_y(u, p)
    rest_x(1)
    far_x(1)
    product(0, 1)
    for p in (0, 2):
            forward_x(3, p)
    for u, p in ((1, 2), (2, 0), (1, 3), (2, 1)):
            forward_y(u, p)
    rest_y(1)
    rest_y(2)
    for p in (1, 3):
            recv_z_last(p, jnp.logical_not(middle))
    for p in (0, 2, 1, 3):
            far_wz(p)
    far_wz_back()
    sum_gradients()
    far_y(1)
    far_y(2)
    rest_x(2)
    far_x(2)
    product(0, 2)
    recv_c(1)
    product(1, 0)
    for p in (0, 2, 1, 3):
            forward_y(3, p)
    for p in (1, 3):
            forward_x(3, p)
    product(1, 1)
    product(1, 2)
    importance()
    rest_y(3)
    far_y(3)
    recv_c(2)
    product(2, 0)
    product(2, 1)
    product(2, 2)
    rest_x(3)
    far_x(3)
    product(0, 3)
    product(1, 3)
    product(2, 3)
    recv_c(3)
    product(3, 0)
    product(3, 1)
    product(3, 2)
    product(3, 3)
    proj[...] = acc[...].astype(jnp.bfloat16)
    stores[3].start()

    for copy in sends:
        copy.wait_send()
    for cond, copy in z_forwards:

        @pl.when(cond)
        def _(copy=copy):
            copy.wait_send()

    @pl.when(jnp.logical_not(off_diagonal))
    def _():
        down_away.wait_send()

    @pl.when(off_diagonal)
    def _():
        for copy in down_mirror:
            copy.wait_send()
        gradient_copy().wait_send()

    for store in stores:
        store.wait()


def local(tokens, weight, down, up, cotangent, importance):
    bf16, f32 = jnp.bfloat16, jnp.float32
    dma = pltpu.SemaphoreType.DMA
    return pl.pallas_call(
        kernel,
        out_shape=(
            jax.ShapeDtypeStruct((512, 512), bf16),
            jax.ShapeDtypeStruct((8, 512), f32),
            jax.ShapeDtypeStruct((8, 256), f32),
            jax.ShapeDtypeStruct((256, 512), f32),
        ),
        in_specs=[
            pl.BlockSpec(memory_space=pltpu.VMEM if i in (2, 3) else pltpu.HBM) for i in range(6)
        ],
        out_specs=[pl.BlockSpec(memory_space=pl.ANY)] * 4,
        scratch_shapes=[
            pltpu.VMEM((4, 4, 512, 512), bf16),
            pltpu.VMEM((4, 4, 2, 256, 512), bf16),
            pltpu.VMEM((512, 512), f32),
            pltpu.VMEM((512, 512), bf16),
            pltpu.VMEM((512, 512), bf16),
            pltpu.VMEM((256, 512), f32),
            pltpu.VMEM((256, 512), f32),
            pltpu.VMEM((8, 512), f32),
            pltpu.VMEM((8, 256), f32),
            pltpu.VMEM((2, 8, 256), f32),
            pltpu.VMEM((3, 8, 256), f32),
            pltpu.VMEM((4, 16, 512), f32),
            pltpu.VMEM((4, 16, 512), f32),
            pltpu.VMEM((2, 16, 512), f32),
            pltpu.VMEM((4, 16, 512), f32),
            pltpu.VMEM((4, 16, 512), f32),
            dma((4,)), dma((4,)),
            dma((2, 4, 4)), dma((2, 4, 4)), dma((4, 4)), dma((4, 4)), dma((2, 4, 4)), dma((4, 4)),
            dma((2, 4)), dma((2, 4)), dma((4,)), dma((4,)),
            dma((2, 4, 4)), dma((2, 4, 4)), dma((4, 4)), dma((4, 4)), dma((4, 4, 2)), dma((4, 4, 2)),
            dma((3,)), dma((4,)), dma((3,)), dma((4,)), dma((1,)), dma((2,)),
            dma((3,)), dma((4,)), dma((3,)), dma((4,)),
            dma((3,)), dma((2,)), dma, dma,
        ],
        compiler_params=pltpu.CompilerParams(
            collective_id=0, has_side_effects=True, vmem_limit_bytes=63 * 2**20
        ),
    )(tokens, weight, down, up, cotangent, importance)


def solution(mesh):
    placed = (
        P("fsdp", "tp"),
        P("fsdp", "tp"),
        P(None, "fsdp"),
        P(None, "tp"),
        P("fsdp", "tp"),
        P("fsdp", "tp"),
    )
    return jax.shard_map(
        local,
        mesh=mesh,
        in_specs=placed,
        out_specs=(P("fsdp", "tp"), P(None, "tp"), P(None, "fsdp"), P("fsdp", "tp")),
        check_vma=False,
    )
```

```python
import jax
import jax.numpy as jnp
from jax import lax
from jax.experimental import pallas as pl
from jax.experimental.pallas import tpu as pltpu
from jax.sharding import PartitionSpec as P

adapter_scale = 2.0
decay_rate = 0.8
MESH = pl.DeviceIdType.MESH


def dot(a, b, dims, precision=None):
    return lax.dot_general(
        a, b, (dims, ((), ())), preferred_element_type=jnp.float32, precision=precision
    )


def kernel(
    tok_in, w_in, down, up, cot_in, imp_in,
    proj_out, upg_out, dng_out, newimp_out,
    T, W, acc, proj, cot, imp, newimp, upg, dng, down_t, dtot,
    arx, arz, arc, ary, arh,
    load_sem, store_sem,
    tx_s, tx_r, txh_s, txh_r, tz_s, tz_r,
    wz_s, wz_r, wzh_s, wzh_r, wy_s, wy_r, wyh_s, wyh_r, wc_s, wc_r,
    arx_s, arx_r, arz_s, arz_r, arc_s, arc_r, ary_s, ary_r, arh_s, arh_r,
    dt_s, dt_r, dg_s, dg_r,
):
    f = lax.axis_index("fsdp")
    t = lax.axis_index("tp")
    chip = f // 2
    c = f % 2
    y, zh = chip // 4, chip % 4
    x, zl = t // 4, t % 4

    def dev(y=y, zh=zh, c=c, x=x, zl=zl):
        return {"fsdp": (y * 4 + zh) * 2 + c, "tp": x * 4 + zl}

    def ring(i, d):
        return (i + d + 4) % 4

    x_next, x_prev = dev(x=ring(x, 1)), dev(x=ring(x, -1))
    y_next, y_prev = dev(y=ring(y, 1)), dev(y=ring(y, -1))
    h_next, h_prev = dev(zh=ring(zh, 1)), dev(zh=ring(zh, -1))
    l_next, l_prev = dev(zl=ring(zl, 1)), dev(zl=ring(zl, -1))
    sibling = dev(c=1 - c)
    off_diagonal = chip != t

    def mirror(core):
        return {"fsdp": t * 2 + core, "tp": chip}

    def remote(src, dst, send, recv, to):
        return pltpu.make_async_remote_copy(
            src_ref=src, dst_ref=dst, send_sem=send, recv_sem=recv, device_id=to, device_id_type=MESH
        )

    loads = [
        pltpu.make_async_copy(src, dst, load_sem.at[i])
        for i, (src, dst) in enumerate(
            [
                (tok_in, T.at[x, zl]),
                (w_in, W.at[y, zh, c]),
                (cot_in, cot),
                (imp_in, imp),
            ]
        )
    ]
    for load in loads:
        load.start()

    barrier = pltpu.get_barrier_semaphore()
    for r in (1, 2, 3):
        for partner in (dev(x=ring(x, r)), dev(y=ring(y, r)), dev(zh=ring(zh, r)), dev(zl=ring(zl, r))):
            pl.semaphore_signal(barrier, inc=1, device_id=partner, device_id_type=MESH)
    pl.semaphore_signal(barrier, inc=1, device_id=sibling, device_id_type=MESH)

    @pl.when(off_diagonal)
    def _():
        for core in (0, 1):
            pl.semaphore_signal(barrier, inc=1, device_id=mirror(core), device_id_type=MESH)

    for load in loads[:2]:
        load.wait()
    down_f32 = down[...].astype(jnp.float32)
    dtot[2] = down_f32
    pl.semaphore_wait(barrier, jnp.where(off_diagonal, 15, 13))

    sends = []

    def go(copy):
        copy.start()
        sends.append(copy)
        return copy

    def go_later(copy):
        sends.append(copy)
        return copy

    down_away = remote(dtot.at[2], down_t.at[c], dt_s.at[0], dt_r.at[c], sibling)
    down_mirror = [
        remote(dtot.at[2], down_t.at[c], dt_s.at[1 + core], dt_r.at[c], mirror(core)) for core in (0, 1)
    ]

    @pl.when(jnp.logical_not(off_diagonal))
    def _():
        down_t[c] = down_f32
        down_away.start()

    @pl.when(off_diagonal)
    def _():
        for copy in down_mirror:
            copy.start()

    unit = [
        zl,
        jnp.where(zl == 0, 1, jnp.where(zl == 1, 0, jnp.where(zl == 2, 1, 2))),
        jnp.where(zl == 0, 2, jnp.where(zl == 1, 2, jnp.where(zl == 2, 3, 1))),
        jnp.where(zl < 2, 3, 0),
    ]
    wunit = [zh, ring(zh, -1), ring(zh, 1), ring(zh, 2)]

    def rows(p, size):
        return pl.ds(p * size, size)

    def recv(dst, sem):
        remote(dst, dst, sem, sem, sibling).wait_recv()

    tp, wp = 128, 64

    def send_x(j, p, sides=(0, 1)):
        block = T.at[x, unit[j], rows(p, tp)]
        for side in sides:
            to = (x_next, x_prev)[side]
            go(remote(block, block, tx_s.at[side, j, p], tx_r.at[side, j, p], to))

    z_forwards = []
    z_last = []

    def send_z(j, p):
        block = T.at[x, unit[j], rows(p, tp)]
        if j == 0:
            cases = ((zl < 3, l_next, 0), (zl > 0, l_prev, 1))
        else:
            cases = (
                (jnp.logical_and(unit[j] < zl, zl < 3), l_next, 0),
                (jnp.logical_and(unit[j] > zl, zl > 0), l_prev, 1),
            )
        for cond, to, side in cases:
            copy = remote(block, block, tz_s.at[side, j, p], tz_r.at[unit[j], p], to)
            z_forwards.append((cond, copy))

            @pl.when(cond)
            def _(copy=copy):
                copy.start()

    def recv_z(j, p):
        recv(T.at[x, unit[j], rows(p, tp)], tz_r.at[unit[j], p])
        send_z(j, p)
        send_x(j, p)

    middle = jnp.logical_and(zl > 0, zl < 3)
    last_x = {}

    def recv_z_last(p, here):
        block = T.at[x, unit[3], rows(p, tp)]
        first = p not in last_x
        if first:
            last_x[p] = [
                go_later(remote(block, block, tx_s.at[side, 3, p], tx_r.at[side, 3, p], to))
                for side, to in enumerate((x_next, x_prev))
            ]
            for cond, to, side in (
                (jnp.logical_and(unit[3] < zl, zl < 3), l_next, 0),
                (jnp.logical_and(unit[3] > zl, zl > 0), l_prev, 1),
            ):
                copy = remote(block, block, tz_s.at[side, 3, p], tz_r.at[unit[3], p], to)
                z_forwards.append((cond, copy))
                z_last.append((p, cond, copy))

        @pl.when(here)
        def _():
            recv(block, tz_r.at[unit[3], p])
            for q, cond, copy in z_last:
                if q == p and first:
                    pl.when(cond)(copy.start)
            for copy in last_x[p]:
                copy.start()

    def forward_x(j, p):
        side = p // 2
        near, to = (ring(x, -1), x_next) if side == 0 else (ring(x, 1), x_prev)
        block = T.at[near, unit[j], rows(p, tp)]
        recv(block, tx_r.at[side, j, p])
        go(remote(block, block, txh_s.at[j, p], txh_r.at[j, p], to))

    def rest_x(j):
        for p in (2, 3):
            recv(T.at[ring(x, -1), unit[j], rows(p, tp)], tx_r.at[0, j, p])
        for p in (0, 1):
            recv(T.at[ring(x, 1), unit[j], rows(p, tp)], tx_r.at[1, j, p])

    def far_x(j):
        for p in range(4):
            recv(T.at[ring(x, 2), unit[j], rows(p, tp)], txh_r.at[j, p])

    def core_parts(u):
        return (pl.ds(0, 128), pl.ds(128, 128)) if u == 3 else (pl.ds(0, 256),)

    def send_c(u, r, part=0):
        block = W.at[ring(y, r), wunit[u], c, core_parts(u)[part]]
        go(remote(block, block, wc_s.at[u, r % 4, part], wc_r.at[u, r % 4, part], sibling))

    def recv_c(u):
        for r in range(4):
            for part, where in enumerate(core_parts(u)):
                recv(W.at[ring(y, r), wunit[u], 1 - c, where], wc_r.at[u, r, part])

    def send_y(u, p, sides=(0, 1)):
        block = W.at[y, wunit[u], c, rows(p, wp)]
        for side in sides:
            to = (y_next, y_prev)[side]
            go(remote(block, block, wy_s.at[side, u, p], wy_r.at[side, u, p], to))

    def forward_y(u, p):
        side = p // 2
        near, to = (ring(y, -1), y_next) if side == 0 else (ring(y, 1), y_prev)
        block = W.at[near, wunit[u], c, rows(p, wp)]
        recv(block, wy_r.at[side, u, p])
        go(remote(block, block, wyh_s.at[u, p], wyh_r.at[u, p], to))
        if u == 3 and p % 2 == 1:
            send_c(u, -1 if side == 0 else 1, side)

    def rest_y(u):
        for p in (2, 3):
            recv(W.at[ring(y, -1), wunit[u], c, rows(p, wp)], wy_r.at[0, u, p])
        send_c(u, -1, len(core_parts(u)) - 1)
        for p in (0, 1):
            recv(W.at[ring(y, 1), wunit[u], c, rows(p, wp)], wy_r.at[1, u, p])
        send_c(u, 1)

    def far_y(u):
        for p in range(4):
            recv(W.at[ring(y, 2), wunit[u], c, rows(p, wp)], wyh_r.at[u, p])
            if u == 3 and p == 1:
                send_c(u, 2)
        send_c(u, 2, len(core_parts(u)) - 1)

    def send_wz(k):
        for q in (0, 1):
            for side, to in enumerate((h_next, h_prev)):
                p = 2 * (k if side == 0 else 1 - k) + q
                block = W.at[y, zh, c, rows(p, wp)]
                go(remote(block, block, wz_s.at[side, p], wz_r.at[side, p], to))

    def forward_wz(p):
        side = p // 2
        near, to = (wunit[1], h_next) if side == 0 else (wunit[2], h_prev)
        block = W.at[y, near, c, rows(p, wp)]
        recv(block, wz_r.at[side, p])
        go(remote(block, block, wzh_s.at[p], wzh_r.at[p], to))
        send_y(1 + side, p)

    def rest_wz(p):
        u = 1 if p >= 2 else 2
        recv(W.at[y, wunit[u], c, rows(p, wp)], wz_r.at[u - 1, p])
        send_y(u, p)
        if p % 2 == 1:
            send_c(u, 0)

    def far_wz(p):
        recv(W.at[y, wunit[3], c, rows(p, wp)], wzh_r.at[p])
        send_y(3, p, (p // 2,))
        if p % 2 == 1:
            send_c(3, 0, p // 2)

    def far_wz_back():
        for p in (0, 2, 1, 3):
            send_y(3, p, (1 - p // 2,))

    def sum_send(buf, me, s, r, to):
        for d in range(1, len(to) + 1):
            go(remote(buf.at[me], buf.at[me], s.at[d - 1], r.at[me], to[d - 1]))

    def sum_recv(buf, me, r, n):
        for d in range(1, n):
            other = (me + d) % n
            recv(buf.at[other], r.at[other])
        total = buf[0] + buf[1]
        for i in range(2, n):
            total = total + buf[i]
        return total

    for p in (0, 1):
        send_x(0, p, (0,))
        send_x(0, 2 + p, (1,))
    for p in (0, 2, 1, 3):
        send_z(0, p)
    for p in (0, 1):
        send_y(0, p, (0,))
        send_y(0, 2 + p, (1,))
    for p in (0, 1):
        send_y(0, 2 + p, (0,))
        send_y(0, p, (1,))
    send_c(0, 0)
    for load in loads[2:]:
        load.wait()

    @pl.when(off_diagonal)
    def _():
        recv(down_t.at[c], dt_r.at[c])

    recv(down_t.at[1 - c], dt_r.at[1 - c])
    down_columns = jnp.concatenate([down_t[0], down_t[1]], axis=1).astype(jnp.bfloat16)
    arx[x, 0:8] = dot(down_columns, T[x, zl], ((1,), (1,)))
    arx[x, 8:16] = dot(up[...], cot[...], ((1,), (1,)))
    sum_send(arx, x, arx_s, arx_r, [dev(x=ring(x, d)) for d in (1, 2, 3)])
    for p in (0, 1):
        send_x(0, 2 + p, (0,))
        send_x(0, p, (1,))

    def sum_low():
        arz[zl] = sum_recv(arx, x, arx_r, 4)
        sum_send(arz, zl, arz_s, arz_r, [dev(zl=ring(zl, d)) for d in (1, 2, 3)])

    def factor_terms():
        both = sum_recv(arz, zl, arz_r, 4)
        low, back = both[0:8].astype(jnp.bfloat16), both[8:16].astype(jnp.bfloat16)
        arc[c, 0:8] = adapter_scale * dot(low, cot[...], ((1,), (0,)))
        arc[c, 8:16] = adapter_scale * dot(back, T[x, zl], ((1,), (0,)))
        sum_send(arc, c, arc_s, arc_r, [sibling])
        acc[...] = adapter_scale * dot(low, up[...], ((0,), (0,)))

    def sum_cores():
        ary[y] = sum_recv(arc, c, arc_r, 2)
        sum_send(ary, y, ary_s, ary_r, [dev(y=ring(y, d)) for d in (1, 2, 3)])

    def sum_y():
        arh[zh] = sum_recv(ary, y, ary_r, 4)
        sum_send(arh, zh, arh_s, arh_r, [dev(zh=ring(zh, d)) for d in (1, 2, 3)])

    def gradient_copy():
        return remote(dtot.at[c], dng, dg_s, dg_r, mirror(c))

    def sum_gradients():
        grads = sum_recv(arh, zh, arh_r, 4)
        upg[...] = grads[0:8]
        dtot[0] = grads[8:16, 0:256]
        dtot[1] = grads[8:16, 256:512]

        @pl.when(off_diagonal)
        def _():
            gradient_copy().start()

        @pl.when(jnp.logical_not(off_diagonal))
        def _():
            dng[...] = dtot[c]

    stores = [
        pltpu.make_async_copy(src, dst, store_sem.at[i])
        for i, (src, dst) in enumerate(
            [(upg, upg_out), (dng, dng_out), (newimp, newimp_out), (proj, proj_out)]
        )
    ]

    def importance():
        @pl.when(off_diagonal)
        def _():
            gradient_copy().wait_recv()

        stores[0].start()
        stores[1].start()
        highest = lax.Precision.HIGHEST
        own_down = down[...]
        estimate = dot(dng[...], up[...].astype(jnp.float32), ((0,), (0,)), highest)
        estimate = estimate + dot(own_down.astype(jnp.float32), upg[...], ((0,), (0,)), highest)
        merged = W[y, zh, c].astype(jnp.float32) + adapter_scale * dot(own_down, up[...], ((0,), (0,)))
        newimp[...] = decay_rate * imp[...] + (1.0 - decay_rate) * jnp.abs(merged * estimate)
        stores[2].start()

    def product(u, j):
        @pl.when(unit[j] == wunit[u])
        def _():
            @pl.loop(0, 2)
            def _(r):
                chunk = pl.ds(pl.multiple_of(r * 256, 256), 256)
                total = acc[chunk]
                for i in range(4):
                    weights = W[i, wunit[u]].reshape(512, 512)
                    total = total + dot(T[i, wunit[u], chunk], weights, ((1,), (0,)))
                acc[chunk] = total

    recv_z(1, 0)
    sum_low()
    recv_z(1, 2)
    recv_z(1, 1)
    recv_z(1, 3)
    for p in (0, 2, 1, 3):
            forward_x(0, p)
    for p in (0, 2, 1, 3):
            recv_z(2, p)
    send_wz(0)
    for p in (0, 2):
            recv_z_last(p, middle)
    send_wz(1)
    for p in (0, 2, 1, 3):
            forward_y(0, p)
    factor_terms()
    for p in (0, 2, 1, 3):
            forward_x(1, p)
    sum_cores()
    rest_y(0)
    far_y(0)
    rest_x(0)
    far_x(0)
    recv_c(0)
    product(0, 0)
    for p in (0, 2, 1, 3):
            forward_wz(p)
    for p in (1, 3):
            recv_z_last(p, middle)
    for p in (0, 2, 1, 3):
            forward_x(2, p)
    for p in (0, 2):
            recv_z_last(p, jnp.logical_not(middle))
    sum_y()
    for p in (0, 2, 1, 3):
            rest_wz(p)
    for u, p in ((1, 0), (2, 2), (1, 1), (2, 3)):
            forward_y(u, p)
    rest_x(1)
    far_x(1)
    product(0, 1)
    for p in (0, 2):
            forward_x(3, p)
    for u, p in ((1, 2), (2, 0), (1, 3), (2, 1)):
            forward_y(u, p)
    rest_y(1)
    rest_y(2)
    for p in (1, 3):
            recv_z_last(p, jnp.logical_not(middle))
    for p in (0, 2, 1, 3):
            far_wz(p)
    far_wz_back()
    sum_gradients()
    far_y(1)
    far_y(2)
    rest_x(2)
    far_x(2)
    product(0, 2)
    recv_c(1)
    product(1, 0)
    for p in (0, 2, 1, 3):
            forward_y(3, p)
    for p in (1, 3):
            forward_x(3, p)
    product(1, 1)
    product(1, 2)
    importance()
    recv_c(2)
    product(2, 0)
    product(2, 1)
    product(2, 2)
    rest_y(3)
    far_y(3)
    rest_x(3)
    far_x(3)
    product(0, 3)
    product(1, 3)
    product(2, 3)
    recv_c(3)
    product(3, 0)
    product(3, 1)
    product(3, 2)
    product(3, 3)
    proj[...] = acc[...].astype(jnp.bfloat16)
    stores[3].start()

    for copy in sends:
        copy.wait_send()
    for cond, copy in z_forwards:

        @pl.when(cond)
        def _(copy=copy):
            copy.wait_send()

    @pl.when(jnp.logical_not(off_diagonal))
    def _():
        down_away.wait_send()

    @pl.when(off_diagonal)
    def _():
        for copy in down_mirror:
            copy.wait_send()
        gradient_copy().wait_send()

    for store in stores:
        store.wait()


def local(tokens, weight, down, up, cotangent, importance):
    bf16, f32 = jnp.bfloat16, jnp.float32
    dma = pltpu.SemaphoreType.DMA
    return pl.pallas_call(
        kernel,
        out_shape=(
            jax.ShapeDtypeStruct((512, 512), bf16),
            jax.ShapeDtypeStruct((8, 512), f32),
            jax.ShapeDtypeStruct((8, 256), f32),
            jax.ShapeDtypeStruct((256, 512), f32),
        ),
        in_specs=[
            pl.BlockSpec(memory_space=pltpu.VMEM if i in (2, 3) else pltpu.HBM) for i in range(6)
        ],
        out_specs=[pl.BlockSpec(memory_space=pl.ANY)] * 4,
        scratch_shapes=[
            pltpu.VMEM((4, 4, 512, 512), bf16),
            pltpu.VMEM((4, 4, 2, 256, 512), bf16),
            pltpu.VMEM((512, 512), f32),
            pltpu.VMEM((512, 512), bf16),
            pltpu.VMEM((512, 512), bf16),
            pltpu.VMEM((256, 512), f32),
            pltpu.VMEM((256, 512), f32),
            pltpu.VMEM((8, 512), f32),
            pltpu.VMEM((8, 256), f32),
            pltpu.VMEM((2, 8, 256), f32),
            pltpu.VMEM((3, 8, 256), f32),
            pltpu.VMEM((4, 16, 512), f32),
            pltpu.VMEM((4, 16, 512), f32),
            pltpu.VMEM((2, 16, 512), f32),
            pltpu.VMEM((4, 16, 512), f32),
            pltpu.VMEM((4, 16, 512), f32),
            dma((4,)), dma((4,)),
            dma((2, 4, 4)), dma((2, 4, 4)), dma((4, 4)), dma((4, 4)), dma((2, 4, 4)), dma((4, 4)),
            dma((2, 4)), dma((2, 4)), dma((4,)), dma((4,)),
            dma((2, 4, 4)), dma((2, 4, 4)), dma((4, 4)), dma((4, 4)), dma((4, 4, 2)), dma((4, 4, 2)),
            dma((3,)), dma((4,)), dma((3,)), dma((4,)), dma((1,)), dma((2,)),
            dma((3,)), dma((4,)), dma((3,)), dma((4,)),
            dma((3,)), dma((2,)), dma, dma,
        ],
        compiler_params=pltpu.CompilerParams(
            collective_id=0, has_side_effects=True, vmem_limit_bytes=63 * 2**20
        ),
    )(tokens, weight, down, up, cotangent, importance)


def solution(mesh):
    placed = (
        P("fsdp", "tp"),
        P("fsdp", "tp"),
        P(None, "fsdp"),
        P(None, "tp"),
        P("fsdp", "tp"),
        P("fsdp", "tp"),
    )
    return jax.shard_map(
        local,
        mesh=mesh,
        in_specs=placed,
        out_specs=(P("fsdp", "tp"), P(None, "tp"), P(None, "fsdp"), P("fsdp", "tp")),
        check_vma=False,
    )
```
